32 devices in a mesh: grp: 2 (over y), row: 8 (over z, x), col: 2 (over core).
Axes of the slice: x: 2, y: 2, z: 4, core: 2. Of those that a mesh axis runs over, the one named last changes fastest.
Arguments:
- images: bfloat16 [256, 768], P(('grp', 'row', 'col')), parts along dimension 0, may hold values from -0.5 to 0.5
- texts: bfloat16 [256, 768], P(('grp', 'row', 'col')), parts along dimension 0, may hold values from -0.5 to 0.5
- match: int32 [256], P(('grp', 'row', 'col')), parts along dimension 0, may hold values from 0 to 127, as said below
- logit_scale: float32 [1], replicated, may hold values from 6 to 12
- logit_bias: float32 [1], replicated, may hold values from -9 to -6
Outputs:
- loss: float32 [2], P('grp'), parts along dimension 0
- grad_images: float32 [256, 768], P(('grp', 'row', 'col')), parts along dimension 0
- grad_texts: float32 [256, 768], P(('grp', 'row', 'col')), parts along dimension 0
The draws below stay inside these ranges and needn't reach their ends.
There are 2 independent parts, one for each index of `grp`. The reference program is written for one: setup_inputs(seed, part) draws one part's arguments, and reference() takes and returns one part's arrays. A program takes and returns all parts, laid end to end along the dimension named above; an argument that names none is the same for every part. Nothing has to cross between parts.
Inputs may be any that keep to these rules, and one draw needn't show every extreme that they name: match is a permutation of 0 to 127.
All inputs are finite; a program needn't handle non-finite values.
Results may differ from the reference program's by a relative error of at most 0.0051.
Values may be sent and summed in bfloat16 or wider, within the bound.
A program may use at most 64 MiB of HBM per device.

```python
import math
import jax
import jax.numpy as jnp
from jax import lax

D = 768
BATCH = 128


def shared_parts(key):
    order = jax.random.permutation(jax.random.fold_in(key, 11), BATCH).astype(jnp.int32)
    groups = jax.random.randint(jax.random.fold_in(key, 12), (BATCH,), 0, 16)
    centers = jax.random.normal(jax.random.fold_in(key, 13), (16, D), jnp.float32)
    paired = jax.random.normal(jax.random.fold_in(key, 14), (BATCH, D), jnp.float32)
    column = jnp.exp(jax.random.uniform(jax.random.fold_in(key, 15), (D,), jnp.float32, -1.2, 1.2))
    common = jax.random.normal(jax.random.fold_in(key, 16), (D,), jnp.float32)
    return (order, groups, centers, paired, column, common)


def mixed_rows(parts, noise, rows, center_w, pair_w, noise_w):
    order, groups, centers, paired, column, common = parts
    picked = centers[groups]
    mixed = center_w * picked + pair_w * paired + noise_w * noise
    factor = 1.0 / math.sqrt(D * 2.28)
    return jnp.clip(mixed * column[None, :] * rows[:, None] * factor, -0.5, 0.5)


def draw_match(key, part):
    parts = shared_parts(key)
    return parts[0]


def draw_images(key, part):
    parts = shared_parts(key)
    key = jax.random.fold_in(key, 1)
    noise = jax.random.normal(jax.random.fold_in(key, 2), (BATCH, D), jnp.float32)
    rows = jnp.exp(jax.random.uniform(jax.random.fold_in(key, 3), (BATCH,), jnp.float32, -0.9162907, 1.3862944))
    values = mixed_rows(parts, noise, rows, 0.5, 0.7, 0.5)
    return values.astype(jnp.bfloat16)


def draw_texts(key, part):
    parts = shared_parts(key)
    key = jax.random.fold_in(key, 2)
    noise = jax.random.normal(jax.random.fold_in(key, 2), (BATCH, D), jnp.float32)
    rows = jnp.exp(jax.random.uniform(jax.random.fold_in(key, 3), (BATCH,), jnp.float32, -0.9162907, 1.3862944))
    values = mixed_rows(parts, noise, rows, 0.5, 0.7, 0.5)
    placed = jnp.zeros((BATCH, D), jnp.float32).at[parts[0]].set(values)
    return placed.astype(jnp.bfloat16)


def setup_inputs(seed: int = 0, part: int = 0) -> dict:
    splits = jax.random.split(jax.random.key(seed), 6)
    part_splits = jax.random.split(jax.random.fold_in(splits[5], part), 6)
    images = draw_images(jax.random.fold_in(jax.random.fold_in(splits[5], part), 71), part)
    texts = draw_texts(jax.random.fold_in(jax.random.fold_in(splits[5], part), 71), part)
    match = draw_match(jax.random.fold_in(jax.random.fold_in(splits[5], part), 71), part)
    logit_scale = jnp.clip(jax.random.uniform(splits[3], (1,), jnp.float32, 6.0, 12.0), 6.0, 12.0)
    logit_bias = jnp.clip(jax.random.uniform(splits[4], (1,), jnp.float32, -9.0, -6.0), -9.0, -6.0)
    return {"images": images, "texts": texts, "match": match, "logit_scale": logit_scale, "logit_bias": logit_bias}


def unit_rows(values):
    wide = values.astype(jnp.float32)
    norms = jnp.sqrt(lax.optimization_barrier(jnp.sum(wide * wide, axis=1, keepdims=True)) + 1e-06)
    return (wide / norms, norms)

def back_rows(unit, norms, grads):
    inner = lax.optimization_barrier(jnp.sum(unit * grads, axis=1, keepdims=True))
    return (grads - unit * inner) / norms

def reference(images, texts, match, logit_scale, logit_bias):
    scale = logit_scale[0]
    offset = logit_bias[0]
    unit_img, inorm = unit_rows(images)
    unit_txt, tnorm = unit_rows(texts)
    img_b = unit_img.astype(jnp.bfloat16)
    txt_b = unit_txt.astype(jnp.bfloat16)
    logits = scale * jnp.dot(img_b, txt_b.T, preferred_element_type=jnp.float32) + offset
    columns = jnp.arange(texts.shape[0], dtype=jnp.int32)
    label = jnp.where(match[:, None] == columns[None, :], jnp.float32(1.0), jnp.float32(-1.0))
    total = jnp.sum(jax.nn.log_sigmoid(label * logits))
    loss = (-total / BATCH).reshape(1)
    coef = (-label * jax.nn.sigmoid(-label * logits)).astype(jnp.bfloat16)
    gimg = scale * jnp.dot(coef, txt_b, preferred_element_type=jnp.float32)
    gtxt = scale * jnp.dot(coef.T, img_b, preferred_element_type=jnp.float32)
    return (loss, back_rows(unit_img, inorm, gimg), back_rows(unit_txt, tnorm, gtxt))
```

```python
import functools
import jax
import jax.numpy as jnp
from jax import lax
from jax.experimental import pallas as pl
from jax.experimental.pallas import tpu as pltpu
from jax.sharding import PartitionSpec as P

MESH = pl.DeviceIdType.MESH
F32 = jnp.float32
BF16 = jnp.bfloat16


def split_rows(row_count, col_count):
    best = 1
    for low in range(1, row_count + 1):
        if row_count % low == 0:
            if max(low * col_count, row_count // low) < max(best * col_count, row_count // best):
                best = low
    return best


def unit_rows(values):
    wide = values.astype(F32)
    norms = jnp.sqrt(jnp.sum(wide * wide, axis=1, keepdims=True) + 1e-06)
    return (wide / norms, norms)


def back_rows(unit, norms, grads):
    inner = jnp.sum(unit * grads, axis=1, keepdims=True)
    return (grads - unit * inner) / norms


def fold(rows):
    half = rows.shape[1] // 2
    return jnp.concatenate([rows[:, :half], rows[:, half:]], axis=0)


def unfold(blocks):
    n, r2, h = blocks.shape
    r = r2 // 2
    wide = blocks.astype(F32)
    left = wide[:, :r, :].reshape(n * r, h)
    right = wide[:, r:, :].reshape(n * r, h)
    return jnp.concatenate([left, right], axis=1)


def kernel(
    low,
    row_count,
    col_count,
    images_hbm,
    texts_hbm,
    match_hbm,
    scale_hbm,
    bias_hbm,
    loss_ref,
    gimg_ref,
    gtxt_ref,
    images_ref,
    texts_ref,
    match_ref,
    scale_ref,
    bias_ref,
    img_buf,
    txt_buf,
    match_buf,
    img_part,
    txt_part,
    img_back,
    txt_back,
    loss_own,
    loss_buf,
    in_sem,
    img_send,
    img_recv,
    txt_send,
    txt_recv,
    match_send,
    match_recv,
    ipart_send,
    ipart_recv,
    tpart_send,
    tpart_recv,
    loss_send,
    loss_recv,
):
    shard, width = images_ref.shape
    high = row_count // low
    wide = low * col_count
    count = row_count * col_count
    row = lax.axis_index("row")
    col = lax.axis_index("col")
    hi, lo = row // low, row % low
    place = lo * col_count + col

    def at_place(q):
        return {"row": hi * low + q // col_count, "col": q % col_count}

    def at_high(p):
        return {"row": p * low + lo, "col": col}

    loads = [
        pltpu.make_async_copy(src, dst, in_sem.at[n])
        for n, (src, dst) in enumerate(
            [
                (images_hbm, images_ref),
                (texts_hbm, texts_ref),
                (match_hbm, match_ref),
                (scale_hbm, scale_ref),
                (bias_hbm, bias_ref),
            ]
        )
    ]
    for load in loads:
        load.start()

    barrier = pltpu.get_barrier_semaphore()
    for o in range(1, high):
        pl.semaphore_signal(barrier, inc=1, device_id=at_high((hi + o) % high), device_id_type=MESH)
    for o in range(1, wide):
        pl.semaphore_signal(barrier, inc=1, device_id=at_place((place + o) % wide), device_id_type=MESH)

    for load in loads:
        load.wait()
    unit_txt, tnorm = unit_rows(texts_ref[...])
    unit_img, inorm = unit_rows(images_ref[...])
    txt_buf[0] = fold(unit_txt).astype(BF16)
    img_buf[0] = fold(unit_img).astype(BF16)
    sub = lax.broadcasted_iota(jnp.int32, (shard, 128), 0)
    own_match = jnp.zeros((shard, 128), jnp.int32)
    for r in range(shard):
        own_match = jnp.where(sub == r, match_ref[r], own_match)
    match_buf[0] = own_match
    scale = scale_ref[0]
    offset = bias_ref[0]

    pl.semaphore_wait(barrier, high + wide - 2)

    first = []
    for o in range(1, high):
        first.append(
            pltpu.make_async_remote_copy(
                txt_buf.at[0], txt_buf.at[o], txt_send.at[o], txt_recv.at[o],
                device_id=at_high((hi + o) % high), device_id_type=MESH,
            )
        )
    for o in range(1, wide):
        target = at_place((place + o) % wide)
        first.append(
            pltpu.make_async_remote_copy(
                img_buf.at[0], img_buf.at[o], img_send.at[o], img_recv.at[o],
                device_id=target, device_id_type=MESH,
            )
        )
        first.append(
            pltpu.make_async_remote_copy(
                match_buf.at[0], match_buf.at[o], match_send.at[o], match_recv.at[o],
                device_id=target, device_id_type=MESH,
            )
        )
    for copy in first:
        copy.start()
    for copy in first:
        copy.wait_recv()

    img_block = unfold(img_buf[...]).astype(BF16)
    txt_block = unfold(txt_buf[...]).astype(BF16)
    rows, cols = wide * shard, high * shard
    lane = lax.broadcasted_iota(jnp.int32, (rows, cols), 1)
    source = hi - lane // shard
    source = jnp.where(source < 0, source + high, source)
    text_index = (source * wide + place) * shard + lane % shard
    match_block = match_buf[...].reshape(rows, 128)[:, :1]
    label = jnp.where(match_block == text_index, F32(1.0), F32(-1.0))
    logits = (
        scale
        * lax.dot_general(img_block, txt_block, (((1,), (1,)), ((), ())), preferred_element_type=F32)
        + offset
    )
    signed = label * logits
    decay = jnp.exp(-jnp.abs(signed))
    terms = jnp.minimum(signed, 0.0) - jnp.log1p(decay)
    coef = (-label * jnp.where(signed >= 0, decay, 1.0) / (1.0 + decay)).astype(BF16)

    loss_own[...] = jnp.full(loss_own.shape, jnp.sum(terms), F32)

    def loss_copy(o):
        p = place + o % wide
        p = jnp.where(p >= wide, p - wide, p)
        h = hi + o // wide
        h = jnp.where(h >= high, h - high, h)
        target = {"row": h * low + p // col_count, "col": p % col_count}
        return pltpu.make_async_remote_copy(
            loss_own, loss_buf.at[o], loss_send.at[o], loss_recv.at[o],
            device_id=target, device_id_type=MESH,
        )

    second = []
    txt_terms = lax.dot_general(coef, img_block, (((0,), (0,)), ((), ())), preferred_element_type=F32)
    txt_part[...] = txt_terms.reshape(high, shard, width)
    for o in range(1, high):
        second.append(
            pltpu.make_async_remote_copy(
                txt_part.at[o], txt_back.at[o], tpart_send.at[o], tpart_recv.at[o],
                device_id=at_high((hi + high - o) % high), device_id_type=MESH,
            )
        )
        second[-1].start()
    img_terms = jnp.dot(coef, txt_block, preferred_element_type=F32)
    img_part[...] = img_terms.reshape(wide, shard, width)
    for o in range(1, wide):
        second.append(
            pltpu.make_async_remote_copy(
                img_part.at[o], img_back.at[o], ipart_send.at[o], ipart_recv.at[o],
                device_id=at_place((place + wide - o) % wide), device_id_type=MESH,
            )
        )
        second[-1].start()

    if count <= 32:
        for o in range(1, count):
            loss_copy(o).start()
    else:
        lax.fori_loop(1, count, lambda o, c: (loss_copy(o).start(), c)[1], 0)

    for copy in second:
        copy.wait_recv()
    gimg = img_part[0]
    for o in range(1, wide):
        gimg = gimg + img_back[o]
    gimg_ref[...] = back_rows(unit_img, inorm, scale * gimg)
    gtxt = txt_part[0]
    for o in range(1, high):
        gtxt = gtxt + txt_back[o]
    gtxt_ref[...] = back_rows(unit_txt, tnorm, scale * gtxt)

    loss_buf[0] = loss_own[...]
    if count <= 32:
        for o in range(1, count):
            loss_copy(o).wait_recv()
    else:
        lax.fori_loop(1, count, lambda o, c: (loss_copy(o).wait_recv(), c)[1], 0)
    total = jnp.sum(loss_buf[...], axis=0)
    loss_ref[0] = -total[0, 0] / (shard * count)

    for copy in first + second:
        copy.wait_send()
    if count <= 32:
        for o in range(1, count):
            loss_copy(o).wait_send()
    else:
        lax.fori_loop(1, count, lambda o, c: (loss_copy(o).wait_send(), c)[1], 0)


def body(images, texts, match, logit_scale, logit_bias):
    row_count = lax.axis_size("row")
    col_count = lax.axis_size("col")
    low = split_rows(row_count, col_count)
    high = row_count // low
    wide = low * col_count
    count = row_count * col_count
    shard, width = images.shape
    dma = pltpu.SemaphoreType.DMA
    return tuple(
        pl.pallas_call(
            functools.partial(kernel, low, row_count, col_count),
            out_shape=(
                jax.ShapeDtypeStruct((1,), F32),
                jax.ShapeDtypeStruct((shard, width), F32),
                jax.ShapeDtypeStruct((shard, width), F32),
            ),
            in_specs=[pl.BlockSpec(memory_space=pl.ANY)] * 5,
            out_specs=(
                pl.BlockSpec(memory_space=pltpu.SMEM),
                pl.BlockSpec(memory_space=pltpu.VMEM),
                pl.BlockSpec(memory_space=pltpu.VMEM),
            ),
            scratch_shapes=[
                pltpu.VMEM((shard, width), BF16),
                pltpu.VMEM((shard, width), BF16),
                pltpu.SMEM((shard,), jnp.int32),
                pltpu.SMEM((1,), F32),
                pltpu.SMEM((1,), F32),
                pltpu.VMEM((wide, 2 * shard, width // 2), BF16),
                pltpu.VMEM((high, 2 * shard, width // 2), BF16),
                pltpu.VMEM((wide, shard, 128), jnp.int32),
                pltpu.VMEM((wide, shard, width), F32),
                pltpu.VMEM((high, shard, width), F32),
                pltpu.VMEM((wide, shard, width), F32),
                pltpu.VMEM((high, shard, width), F32),
                pltpu.VMEM((8, 128), F32),
                pltpu.VMEM((count, 8, 128), F32),
                dma((5,)),
                dma((wide,)),
                dma((wide,)),
                dma((high,)),
                dma((high,)),
                dma((wide,)),
                dma((wide,)),
                dma((wide,)),
                dma((wide,)),
                dma((high,)),
                dma((high,)),
                dma((count,)),
                dma((count,)),
            ],
            compiler_params=pltpu.CompilerParams(
                collective_id=0, has_side_effects=True, vmem_limit_bytes=32 * 1024 * 1024
            ),
        )(images, texts, match, logit_scale, logit_bias)
    )


def solution(mesh):
    placed = (
        P(("grp", "row", "col"), None),
        P(("grp", "row", "col"), None),
        P(("grp", "row", "col")),
        P(),
        P(),
    )
    return jax.shard_map(
        body,
        mesh=mesh,
        in_specs=placed,
        out_specs=(P("grp"), P(("grp", "row", "col"), None), P(("grp", "row", "col"), None)),
        check_vma=False,
    )
```

```python
import functools
import jax
import jax.numpy as jnp
from jax import lax
from jax.experimental import pallas as pl
from jax.experimental.pallas import tpu as pltpu
from jax.sharding import PartitionSpec as P

MESH = pl.DeviceIdType.MESH
F32 = jnp.float32
BF16 = jnp.bfloat16


def split_rows(row_count, col_count):
    best = 1
    for low in range(1, row_count + 1):
        if row_count % low == 0:
            if max(low * col_count, row_count // low) < max(best * col_count, row_count // best):
                best = low
    return best


def unit_rows(values):
    wide = values.astype(F32)
    norms = jnp.sqrt(jnp.sum(wide * wide, axis=1, keepdims=True) + 1e-06)
    return (wide / norms, norms)


def back_rows(unit, norms, grads):
    inner = jnp.sum(unit * grads, axis=1, keepdims=True)
    return (grads - unit * inner) / norms


def fold(rows):
    half = rows.shape[1] // 2
    return jnp.concatenate([rows[:, :half], rows[:, half:]], axis=0)


def halves(blocks):
    n, r2, h = blocks.shape
    r = r2 // 2
    wide = blocks.astype(F32)
    return wide[:, :r, :].reshape(n * r, h), wide[:, r:, :].reshape(n * r, h)


def exchange(
    low,
    row_count,
    col_count,
    images_hbm,
    texts_hbm,
    match_hbm,
    scale_hbm,
    bias_hbm,
    grads_ref,
    units_ref,
    norms_ref,
    total_ref,
    images_ref,
    texts_ref,
    match_ref,
    scale_ref,
    bias_ref,
    img_buf,
    txt_buf,
    img_part,
    txt_part,
    img_back,
    txt_back,
    loss_own,
    loss_buf,
    in_sem,
    img_send,
    img_recv,
    txt_send,
    txt_recv,
    ipart_send,
    ipart_recv,
    tpart_send,
    tpart_recv,
    loss_send,
    loss_recv,
):
    shard, width = images_ref.shape
    half = width // 2
    high = row_count // low
    wide = low * col_count
    count = row_count * col_count
    row = lax.axis_index("row")
    col = lax.axis_index("col")
    hi, lo = row // low, row % low
    place = lo * col_count + col

    def at_place(q):
        return {"row": hi * low + q // col_count, "col": q % col_count}

    def at_high(p):
        return {"row": p * low + lo, "col": col}

    barrier = pltpu.get_barrier_semaphore()
    for o in range(1, high):
        pl.semaphore_signal(barrier, inc=1, device_id=at_high((hi + o) % high), device_id_type=MESH)
    for o in range(1, wide):
        pl.semaphore_signal(barrier, inc=1, device_id=at_place((place + o) % wide), device_id_type=MESH)

    loads = [
        pltpu.make_async_copy(src, dst, in_sem.at[n])
        for n, (src, dst) in enumerate(
            [
                (texts_hbm, texts_ref),
                (images_hbm, images_ref),
                (match_hbm, match_ref),
                (scale_hbm, scale_ref),
                (bias_hbm, bias_ref),
            ]
        )
    ]
    for load in loads:
        load.start()
    for load in loads:
        load.wait()
    unit_txt, tnorm = unit_rows(texts_ref[...])
    unit_img, inorm = unit_rows(images_ref[...])
    txt_buf[0] = fold(unit_txt).astype(BF16)
    sub = lax.broadcasted_iota(jnp.int32, (2 * shard, 128), 0)
    index = jnp.zeros((2 * shard, 128), jnp.int32)
    for r in range(shard):
        value = match_ref[r]
        index = jnp.where(sub == r, value // 128, jnp.where(sub == r + shard, value % 128, index))
    img_buf[0] = jnp.concatenate([fold(unit_img), index.astype(F32)], axis=1).astype(BF16)
    scale = scale_ref[0]
    offset = bias_ref[0]

    pl.semaphore_wait(barrier, high + wide - 2)

    first = []
    for o in range(1, high):
        first.append(
            pltpu.make_async_remote_copy(
                txt_buf.at[0], txt_buf.at[o], txt_send.at[o], txt_recv.at[o],
                device_id=at_high((hi + o) % high), device_id_type=MESH,
            )
        )
    for o in range(1, wide):
        first.append(
            pltpu.make_async_remote_copy(
                img_buf.at[0], img_buf.at[o], img_send.at[o], img_recv.at[o],
                device_id=at_place((place + o) % wide), device_id_type=MESH,
            )
        )
    for copy in first:
        copy.start()
    units_ref[0] = unit_img
    units_ref[1] = unit_txt
    norms_ref[0] = jnp.broadcast_to(inorm, (shard, 128))
    norms_ref[1] = jnp.broadcast_to(tnorm, (shard, 128))
    rows, cols = wide * shard, high * shard
    lane = lax.broadcasted_iota(jnp.int32, (rows, cols), 1)
    source = hi - lane // shard
    source = jnp.where(source < 0, source + high, source)
    text_index = ((source * wide + place) * shard + lane % shard).astype(F32)
    for copy in first:
        copy.wait_recv()

    left, right = halves(img_buf[...])
    img_block = jnp.concatenate([left[:, :half], right[:, :half]], axis=1).astype(BF16)
    match_block = left[:, half : half + 1] * 128.0 + right[:, half : half + 1]
    txt_block = jnp.concatenate(halves(txt_buf[...]), axis=1).astype(BF16)
    label = jnp.where(match_block == text_index, F32(1.0), F32(-1.0))
    logits = (
        scale
        * lax.dot_general(img_block, txt_block, (((1,), (1,)), ((), ())), preferred_element_type=F32)
        + offset
    )
    signed = label * logits
    decay = jnp.exp(-jnp.abs(signed))
    coef = (-label * jnp.where(signed >= 0, decay, 1.0) / (1.0 + decay)).astype(BF16)

    def loss_copy(o):
        p = place + o % wide
        p = jnp.where(p >= wide, p - wide, p)
        h = hi + o // wide
        h = jnp.where(h >= high, h - high, h)
        target = {"row": h * low + p // col_count, "col": p % col_count}
        return pltpu.make_async_remote_copy(
            loss_own, loss_buf.at[o], loss_send.at[o], loss_recv.at[o],
            device_id=target, device_id_type=MESH,
        )

    def each_loss(act):
        if count <= 32:
            for o in range(1, count):
                act(loss_copy(o))
        else:
            lax.fori_loop(1, count, lambda o, c: (act(loss_copy(o)), c)[1], 0)

    terms = jnp.minimum(signed, 0.0) - jnp.log1p(decay)
    loss_own[...] = jnp.broadcast_to(jnp.sum(terms, keepdims=True), (1, 128))
    loss_buf[0] = loss_own[...]
    each_loss(lambda copy: copy.start())

    second = []
    txt_terms = lax.dot_general(coef, img_block, (((0,), (0,)), ((), ())), preferred_element_type=F32)
    txt_own = txt_terms[:shard]
    for o in range(1, high):
        txt_part[o] = txt_terms[o * shard : (o + 1) * shard]
        second.append(
            pltpu.make_async_remote_copy(
                txt_part.at[o], txt_back.at[o], tpart_send.at[o], tpart_recv.at[o],
                device_id=at_high((hi + high - o) % high), device_id_type=MESH,
            )
        )
        second[-1].start()
    img_terms = jnp.dot(coef, txt_block, preferred_element_type=F32)
    img_own = img_terms[:shard]
    for o in range(1, wide):
        img_part[o] = img_terms[o * shard : (o + 1) * shard]
        second.append(
            pltpu.make_async_remote_copy(
                img_part.at[o], img_back.at[o], ipart_send.at[o], ipart_recv.at[o],
                device_id=at_place((place + wide - o) % wide), device_id_type=MESH,
            )
        )
        second[-1].start()

    for copy in second:
        copy.wait_recv()

    def gathered(own, back, n):
        for o in range(1, n):
            own = own + back[o]
        return scale * own

    grads_ref[0] = gathered(img_own, img_back, wide)
    grads_ref[1] = gathered(txt_own, txt_back, high)
    each_loss(lambda copy: copy.wait_recv())
    total_ref[...] = jnp.sum(loss_buf[...], axis=0)

    for copy in first + second:
        copy.wait_send()
    each_loss(lambda copy: copy.wait_send())


def finish(pairs, grads_ref, units_ref, norms_ref, total_ref, loss_ref, gimg_ref, gtxt_ref):
    gimg_ref[...] = back_rows(units_ref[0], norms_ref[0][:, :1], grads_ref[0])
    gtxt_ref[...] = back_rows(units_ref[1], norms_ref[1][:, :1], grads_ref[1])
    loss_ref[...] = -total_ref[0, :1] / pairs


def body(images, texts, match, logit_scale, logit_bias):
    row_count = lax.axis_size("row")
    col_count = lax.axis_size("col")
    low = split_rows(row_count, col_count)
    high = row_count // low
    wide = low * col_count
    count = row_count * col_count
    shard, width = images.shape
    half = width // 2
    dma = pltpu.SemaphoreType.DMA
    vmem = pl.BlockSpec(memory_space=pltpu.VMEM)
    inputs = [pltpu.with_memory_space_constraint(images, pltpu.HBM), pltpu.with_memory_space_constraint(texts, pltpu.HBM), pltpu.with_memory_space_constraint(match, pltpu.HBM), logit_scale, logit_bias]
    sums = pl.pallas_call(
        functools.partial(exchange, low, row_count, col_count),
        out_shape=(
            jax.ShapeDtypeStruct((2, shard, width), F32),
            jax.ShapeDtypeStruct((2, shard, width), F32),
            jax.ShapeDtypeStruct((2, shard, 128), F32),
            jax.ShapeDtypeStruct((1, 128), F32),
        ),
        in_specs=[pl.BlockSpec(memory_space=pl.ANY)] * 5,
        out_specs=(vmem,) * 4,
        scratch_shapes=[
            pltpu.VMEM((shard, width), BF16),
            pltpu.VMEM((shard, width), BF16),
            pltpu.SMEM((shard,), jnp.int32),
            pltpu.SMEM((1,), F32),
            pltpu.SMEM((1,), F32),
            pltpu.VMEM((wide, 2 * shard, half + 128), BF16),
            pltpu.VMEM((high, 2 * shard, half), BF16),
            pltpu.VMEM((wide, shard, width), F32),
            pltpu.VMEM((high, shard, width), F32),
            pltpu.VMEM((wide, shard, width), F32),
            pltpu.VMEM((high, shard, width), F32),
            pltpu.VMEM((1, 128), F32),
            pltpu.VMEM((count, 1, 128), F32),
            dma((5,)),
            dma((wide,)),
            dma((wide,)),
            dma((high,)),
            dma((high,)),
            dma((wide,)),
            dma((wide,)),
            dma((high,)),
            dma((high,)),
            dma((count,)),
            dma((count,)),
        ],
        compiler_params=pltpu.CompilerParams(
            collective_id=0, has_side_effects=True, vmem_limit_bytes=32 * 1024 * 1024
        ),
    )(*inputs)
    return tuple(
        pl.pallas_call(
            functools.partial(finish, shard * count),
            out_shape=(
                jax.ShapeDtypeStruct((1,), F32),
                jax.ShapeDtypeStruct((shard, width), F32),
                jax.ShapeDtypeStruct((shard, width), F32),
            ),
            in_specs=[vmem] * 4,
            out_specs=(vmem,) * 3,
            compiler_params=pltpu.CompilerParams(vmem_limit_bytes=4 * 1024 * 1024),
        )(*sums)
    )


def solution(mesh):
    placed = (
        P(("grp", "row", "col"), None),
        P(("grp", "row", "col"), None),
        P(("grp", "row", "col")),
        P(),
        P(),
    )
    return jax.shard_map(
        body,
        mesh=mesh,
        in_specs=placed,
        out_specs=(P("grp"), P(("grp", "row", "col"), None), P(("grp", "row", "col"), None)),
        check_vma=False,
    )
```

```python
import functools
import jax
import jax.numpy as jnp
from jax import lax
from jax.experimental import pallas as pl
from jax.experimental.pallas import tpu as pltpu
from jax.sharding import PartitionSpec as P

MESH = pl.DeviceIdType.MESH
F32 = jnp.float32
BF16 = jnp.bfloat16


def split_rows(row_count, col_count):
    best = 1
    for low in range(1, row_count + 1):
        if row_count % low == 0:
            if max(low, row_count // low * col_count) < max(best, row_count // best * col_count):
                best = low
    return best


def unit_rows(values):
    wide = values.astype(F32)
    norms = jnp.sqrt(jnp.sum(wide * wide, axis=1, keepdims=True) + 1e-06)
    return (wide / norms, norms)


def back_rows(unit, norms, grads):
    inner = jnp.sum(unit * grads, axis=1, keepdims=True)
    return (grads - unit * inner) / norms


def fold(rows):
    half = rows.shape[1] // 2
    return jnp.concatenate([rows[:, :half], rows[:, half:]], axis=0)


def halves(blocks):
    n, r2, h = blocks.shape
    r = r2 // 2
    wide = blocks.astype(F32)
    return wide[:, :r, :].reshape(n * r, h), wide[:, r:, :].reshape(n * r, h)


def exchange(
    low,
    row_count,
    col_count,
    images_hbm,
    texts_hbm,
    match_hbm,
    scale_hbm,
    bias_hbm,
    grads_ref,
    units_ref,
    norms_ref,
    total_ref,
    images_ref,
    texts_ref,
    match_ref,
    scale_ref,
    bias_ref,
    img_buf,
    txt_buf,
    img_part,
    txt_part,
    img_back,
    txt_back,
    loss_own,
    loss_buf,
    in_sem,
    img_send,
    img_recv,
    txt_send,
    txt_recv,
    ipart_send,
    ipart_recv,
    tpart_send,
    tpart_recv,
    loss_send,
    loss_recv,
):
    shard, width = images_ref.shape
    half = width // 2
    high = row_count // low * col_count
    wide = low
    count = row_count * col_count
    row = lax.axis_index("row")
    col = lax.axis_index("col")
    hi, lo = row // low, row % low
    level = hi * col_count + col

    def at_place(q):
        return {"row": hi * low + q, "col": col}

    def at_high(p):
        return {"row": p // col_count * low + lo, "col": p % col_count}

    barrier = pltpu.get_barrier_semaphore()
    for o in range(1, high):
        pl.semaphore_signal(barrier, inc=1, device_id=at_high((level + o) % high), device_id_type=MESH)
    for o in range(1, wide):
        pl.semaphore_signal(barrier, inc=1, device_id=at_place((lo + o) % wide), device_id_type=MESH)

    loads = [
        pltpu.make_async_copy(src, dst, in_sem.at[n])
        for n, (src, dst) in enumerate(
            [
                (texts_hbm, texts_ref),
                (images_hbm, images_ref),
                (match_hbm, match_ref),
                (scale_hbm, scale_ref),
                (bias_hbm, bias_ref),
            ]
        )
    ]
    for load in loads:
        load.start()
    for load in loads:
        load.wait()
    unit_txt, tnorm = unit_rows(texts_ref[...])
    unit_img, inorm = unit_rows(images_ref[...])
    txt_buf[0] = fold(unit_txt).astype(BF16)
    sub = lax.broadcasted_iota(jnp.int32, (2 * shard, 128), 0)
    index = jnp.zeros((2 * shard, 128), jnp.int32)
    for r in range(shard):
        value = match_ref[r]
        index = jnp.where(sub == r, value // 128, jnp.where(sub == r + shard, value % 128, index))
    img_buf[0] = jnp.concatenate([fold(unit_img), index.astype(F32)], axis=1).astype(BF16)
    scale = scale_ref[0]
    offset = bias_ref[0]

    pl.semaphore_wait(barrier, high + wide - 2)

    first = []
    for o in range(1, high):
        first.append(
            pltpu.make_async_remote_copy(
                txt_buf.at[0], txt_buf.at[o], txt_send.at[o], txt_recv.at[o],
                device_id=at_high((level + o) % high), device_id_type=MESH,
            )
        )
    for o in range(1, wide):
        first.append(
            pltpu.make_async_remote_copy(
                img_buf.at[0], img_buf.at[o], img_send.at[o], img_recv.at[o],
                device_id=at_place((lo + o) % wide), device_id_type=MESH,
            )
        )
    for copy in first:
        copy.start()
    units_ref[0] = unit_img
    units_ref[1] = unit_txt
    norms_ref[0] = jnp.broadcast_to(inorm, (shard, 128))
    norms_ref[1] = jnp.broadcast_to(tnorm, (shard, 128))
    rows, cols = wide * shard, high * shard
    lane = lax.broadcasted_iota(jnp.int32, (rows, cols), 1)
    source = level - lane // shard
    source = jnp.where(source < 0, source + high, source)
    text_index = (source // col_count * low + lo) * col_count + source % col_count
    text_index = (text_index * shard + lane % shard).astype(F32)
    for copy in first:
        copy.wait_recv()

    left, right = halves(img_buf[...])
    img_block = jnp.concatenate([left[:, :half], right[:, :half]], axis=1).astype(BF16)
    match_block = left[:, half : half + 1] * 128.0 + right[:, half : half + 1]
    txt_block = jnp.concatenate(halves(txt_buf[...]), axis=1).astype(BF16)
    label = jnp.where(match_block == text_index, F32(1.0), F32(-1.0))
    logits = (
        scale
        * lax.dot_general(img_block, txt_block, (((1,), (1,)), ((), ())), preferred_element_type=F32)
        + offset
    )
    signed = label * logits
    decay = jnp.exp(-jnp.abs(signed))
    coef = (-label * jnp.where(signed >= 0, decay, 1.0) / (1.0 + decay)).astype(BF16)

    def loss_copy(o):
        p = lo + o % wide
        p = jnp.where(p >= wide, p - wide, p)
        h = level + o // wide
        h = jnp.where(h >= high, h - high, h)
        target = {"row": h // col_count * low + p, "col": h % col_count}
        return pltpu.make_async_remote_copy(
            loss_own, loss_buf.at[o], loss_send.at[o], loss_recv.at[o],
            device_id=target, device_id_type=MESH,
        )

    def each_loss(act):
        if count <= 32:
            for o in range(1, count):
                act(loss_copy(o))
        else:
            lax.fori_loop(1, count, lambda o, c: (act(loss_copy(o)), c)[1], 0)

    terms = jnp.minimum(signed, 0.0) - jnp.log1p(decay)
    loss_own[...] = jnp.broadcast_to(jnp.sum(terms, keepdims=True), (1, 128))
    loss_buf[0] = loss_own[...]
    each_loss(lambda copy: copy.start())

    second = []
    txt_terms = lax.dot_general(coef, img_block, (((0,), (0,)), ((), ())), preferred_element_type=F32)
    txt_own = txt_terms[:shard]
    for o in range(1, high):
        txt_part[o] = txt_terms[o * shard : (o + 1) * shard]
        second.append(
            pltpu.make_async_remote_copy(
                txt_part.at[o], txt_back.at[o], tpart_send.at[o], tpart_recv.at[o],
                device_id=at_high((level + high - o) % high), device_id_type=MESH,
            )
        )
        second[-1].start()
    img_terms = jnp.dot(coef, txt_block, preferred_element_type=F32)
    img_own = img_terms[:shard]
    for o in range(1, wide):
        img_part[o] = img_terms[o * shard : (o + 1) * shard]
        second.append(
            pltpu.make_async_remote_copy(
                img_part.at[o], img_back.at[o], ipart_send.at[o], ipart_recv.at[o],
                device_id=at_place((lo + wide - o) % wide), device_id_type=MESH,
            )
        )
        second[-1].start()

    for copy in second:
        copy.wait_recv()

    def gathered(own, back, n):
        for o in range(1, n):
            own = own + back[o]
        return scale * own

    grads_ref[0] = gathered(img_own, img_back, wide)
    grads_ref[1] = gathered(txt_own, txt_back, high)
    each_loss(lambda copy: copy.wait_recv())
    total_ref[...] = jnp.sum(loss_buf[...], axis=0)

    for copy in first + second:
        copy.wait_send()
    each_loss(lambda copy: copy.wait_send())


def finish(pairs, grads_ref, units_ref, norms_ref, total_ref, loss_ref, gimg_ref, gtxt_ref):
    gimg_ref[...] = back_rows(units_ref[0], norms_ref[0][:, :1], grads_ref[0])
    gtxt_ref[...] = back_rows(units_ref[1], norms_ref[1][:, :1], grads_ref[1])
    loss_ref[...] = -total_ref[0, :1] / pairs


def body(images, texts, match, logit_scale, logit_bias):
    row_count = lax.axis_size("row")
    col_count = lax.axis_size("col")
    low = split_rows(row_count, col_count)
    high = row_count // low * col_count
    wide = low
    count = row_count * col_count
    shard, width = images.shape
    half = width // 2
    dma = pltpu.SemaphoreType.DMA
    vmem = pl.BlockSpec(memory_space=pltpu.VMEM)
    inputs = [pltpu.with_memory_space_constraint(images, pltpu.HBM), pltpu.with_memory_space_constraint(texts, pltpu.HBM), pltpu.with_memory_space_constraint(match, pltpu.HBM), logit_scale, logit_bias]
    sums = pl.pallas_call(
        functools.partial(exchange, low, row_count, col_count),
        out_shape=(
            jax.ShapeDtypeStruct((2, shard, width), F32),
            jax.ShapeDtypeStruct((2, shard, width), F32),
            jax.ShapeDtypeStruct((2, shard, 128), F32),
            jax.ShapeDtypeStruct((1, 128), F32),
        ),
        in_specs=[pl.BlockSpec(memory_space=pl.ANY)] * 5,
        out_specs=(vmem,) * 4,
        scratch_shapes=[
            pltpu.VMEM((shard, width), BF16),
            pltpu.VMEM((shard, width), BF16),
            pltpu.SMEM((shard,), jnp.int32),
            pltpu.SMEM((1,), F32),
            pltpu.SMEM((1,), F32),
            pltpu.VMEM((wide, 2 * shard, half + 128), BF16),
            pltpu.VMEM((high, 2 * shard, half), BF16),
            pltpu.VMEM((wide, shard, width), F32),
            pltpu.VMEM((high, shard, width), F32),
            pltpu.VMEM((wide, shard, width), F32),
            pltpu.VMEM((high, shard, width), F32),
            pltpu.VMEM((1, 128), F32),
            pltpu.VMEM((count, 1, 128), F32),
            dma((5,)),
            dma((wide,)),
            dma((wide,)),
            dma((high,)),
            dma((high,)),
            dma((wide,)),
            dma((wide,)),
            dma((high,)),
            dma((high,)),
            dma((count,)),
            dma((count,)),
        ],
        compiler_params=pltpu.CompilerParams(
            collective_id=0, has_side_effects=True, vmem_limit_bytes=32 * 1024 * 1024
        ),
    )(*inputs)
    return tuple(
        pl.pallas_call(
            functools.partial(finish, shard * count),
            out_shape=(
                jax.ShapeDtypeStruct((1,), F32),
                jax.ShapeDtypeStruct((shard, width), F32),
                jax.ShapeDtypeStruct((shard, width), F32),
            ),
            in_specs=[vmem] * 4,
            out_specs=(vmem,) * 3,
            compiler_params=pltpu.CompilerParams(vmem_limit_bytes=4 * 1024 * 1024),
        )(*sums)
    )


def solution(mesh):
    placed = (
        P(("grp", "row", "col"), None),
        P(("grp", "row", "col"), None),
        P(("grp", "row", "col")),
        P(),
        P(),
    )
    return jax.shard_map(
        body,
        mesh=mesh,
        in_specs=placed,
        out_specs=(P("grp"), P(("grp", "row", "col"), None), P(("grp", "row", "col"), None)),
        check_vma=False,
    )
```

```python
import functools
import jax
import jax.numpy as jnp
from jax import lax
from jax.experimental import pallas as pl
from jax.experimental.pallas import tpu as pltpu
from jax.sharding import PartitionSpec as P

MESH = pl.DeviceIdType.MESH
F32 = jnp.float32
BF16 = jnp.bfloat16


def split_rows(row_count, col_count):
    best = 1
    for low in range(1, row_count + 1):
        if row_count % low == 0:
            if max(low, row_count // low * col_count) < max(best, row_count // best * col_count):
                best = low
    return best


def far_first(n):
    return sorted(range(1, n), key=lambda o: abs(o - n // 2))


def unit_rows(values):
    wide = values.astype(F32)
    norms = jnp.sqrt(jnp.sum(wide * wide, axis=1, keepdims=True) + 1e-06)
    return (wide / norms, norms)


def back_rows(unit, norms, grads):
    inner = jnp.sum(unit * grads, axis=1, keepdims=True)
    return (grads - unit * inner) / norms


def fold(rows):
    half = rows.shape[1] // 2
    return jnp.concatenate([rows[:, :half], rows[:, half:]], axis=0)


def halves(blocks):
    n, r2, h = blocks.shape
    r = r2 // 2
    wide = blocks.astype(F32)
    return wide[:, :r, :].reshape(n * r, h), wide[:, r:, :].reshape(n * r, h)


def exchange(
    low,
    row_count,
    col_count,
    images_hbm,
    texts_hbm,
    match_hbm,
    scale_hbm,
    bias_hbm,
    grads_ref,
    units_ref,
    norms_ref,
    total_ref,
    images_ref,
    texts_ref,
    match_ref,
    scale_ref,
    bias_ref,
    img_buf,
    txt_buf,
    img_part,
    txt_part,
    img_back,
    txt_back,
    loss_own,
    loss_buf,
    in_sem,
    img_send,
    img_recv,
    txt_send,
    txt_recv,
    ipart_send,
    ipart_recv,
    tpart_send,
    tpart_recv,
    loss_send,
    loss_recv,
):
    shard, width = images_ref.shape
    half = width // 2
    high = row_count // low * col_count
    wide = low
    count = row_count * col_count
    row = lax.axis_index("row")
    col = lax.axis_index("col")
    hi, lo = row // low, row % low
    level = hi * col_count + col

    def at_place(q):
        return {"row": hi * low + q, "col": col}

    def at_high(p):
        return {"row": p // col_count * low + lo, "col": p % col_count}

    barrier = pltpu.get_barrier_semaphore()
    for o in range(1, high):
        pl.semaphore_signal(barrier, inc=1, device_id=at_high((level + o) % high), device_id_type=MESH)
    for o in range(1, wide):
        pl.semaphore_signal(barrier, inc=1, device_id=at_place((lo + o) % wide), device_id_type=MESH)

    loads = [
        pltpu.make_async_copy(src, dst, in_sem.at[n])
        for n, (src, dst) in enumerate(
            [
                (texts_hbm, texts_ref),
                (images_hbm, images_ref),
                (match_hbm, match_ref),
                (scale_hbm, scale_ref),
                (bias_hbm, bias_ref),
            ]
        )
    ]
    for load in loads:
        load.start()
    for load in loads:
        load.wait()
    unit_txt, tnorm = unit_rows(texts_ref[...])
    unit_img, inorm = unit_rows(images_ref[...])
    txt_buf[0] = fold(unit_txt).astype(BF16)
    sub = lax.broadcasted_iota(jnp.int32, (2 * shard, 128), 0)
    index = jnp.zeros((2 * shard, 128), jnp.int32)
    for r in range(shard):
        value = match_ref[r]
        index = jnp.where(sub == r, value // 128, jnp.where(sub == r + shard, value % 128, index))
    img_buf[0] = jnp.concatenate([fold(unit_img), index.astype(F32)], axis=1).astype(BF16)
    scale = scale_ref[0]
    offset = bias_ref[0]

    pl.semaphore_wait(barrier, high + wide - 2)

    first = []
    for o in far_first(high):
        first.append(
            pltpu.make_async_remote_copy(
                txt_buf.at[0], txt_buf.at[o], txt_send.at[o], txt_recv.at[o],
                device_id=at_high((level + o) % high), device_id_type=MESH,
            )
        )
    for o in far_first(wide):
        first.append(
            pltpu.make_async_remote_copy(
                img_buf.at[0], img_buf.at[o], img_send.at[o], img_recv.at[o],
                device_id=at_place((lo + o) % wide), device_id_type=MESH,
            )
        )
    for copy in first:
        copy.start()
    units_ref[0] = unit_img
    units_ref[1] = unit_txt
    norms_ref[0] = jnp.broadcast_to(inorm, (shard, 128))
    norms_ref[1] = jnp.broadcast_to(tnorm, (shard, 128))
    rows, cols = wide * shard, high * shard
    lane = lax.broadcasted_iota(jnp.int32, (rows, cols), 1)
    source = level - lane // shard
    source = jnp.where(source < 0, source + high, source)
    text_index = (source // col_count * low + lo) * col_count + source % col_count
    text_index = (text_index * shard + lane % shard).astype(F32)
    for copy in first:
        copy.wait_recv()

    left, right = halves(img_buf[...])
    img_block = jnp.concatenate([left[:, :half], right[:, :half]], axis=1).astype(BF16)
    match_block = left[:, half : half + 1] * 128.0 + right[:, half : half + 1]
    txt_block = jnp.concatenate(halves(txt_buf[...]), axis=1).astype(BF16)
    label = jnp.where(match_block == text_index, F32(1.0), F32(-1.0))
    logits = (
        scale
        * lax.dot_general(img_block, txt_block, (((1,), (1,)), ((), ())), preferred_element_type=F32)
        + offset
    )
    signed = label * logits
    decay = jnp.exp(-jnp.abs(signed))
    coef = (-label * jnp.where(signed >= 0, decay, 1.0) / (1.0 + decay)).astype(BF16)

    def loss_copy(o):
        p = lo + o % wide
        p = jnp.where(p >= wide, p - wide, p)
        h = level + o // wide
        h = jnp.where(h >= high, h - high, h)
        target = {"row": h // col_count * low + p, "col": h % col_count}
        return pltpu.make_async_remote_copy(
            loss_own, loss_buf.at[o], loss_send.at[o], loss_recv.at[o],
            device_id=target, device_id_type=MESH,
        )

    def each_loss(act):
        if count <= 32:
            for o in range(1, count):
                act(loss_copy(o))
        else:
            lax.fori_loop(1, count, lambda o, c: (act(loss_copy(o)), c)[1], 0)

    terms = jnp.minimum(signed, 0.0) - jnp.log1p(decay)
    loss_own[...] = jnp.broadcast_to(jnp.sum(terms, keepdims=True), (1, 128))
    loss_buf[0] = loss_own[...]
    each_loss(lambda copy: copy.start())

    second = []
    txt_terms = lax.dot_general(coef, img_block, (((0,), (0,)), ((), ())), preferred_element_type=F32)
    txt_own = txt_terms[:shard]
    for o in far_first(high):
        txt_part[o] = txt_terms[o * shard : (o + 1) * shard]
        second.append(
            pltpu.make_async_remote_copy(
                txt_part.at[o], txt_back.at[o], tpart_send.at[o], tpart_recv.at[o],
                device_id=at_high((level + high - o) % high), device_id_type=MESH,
            )
        )
        second[-1].start()
    img_terms = jnp.dot(coef, txt_block, preferred_element_type=F32)
    img_own = img_terms[:shard]
    for o in far_first(wide):
        img_part[o] = img_terms[o * shard : (o + 1) * shard]
        second.append(
            pltpu.make_async_remote_copy(
                img_part.at[o], img_back.at[o], ipart_send.at[o], ipart_recv.at[o],
                device_id=at_place((lo + wide - o) % wide), device_id_type=MESH,
            )
        )
        second[-1].start()


    def gathered(own, back, n):
        for o in range(1, n):
            own = own + back[o]
        return scale * own

    for copy in second[: high - 1]:
        copy.wait_recv()
    grads_ref[1] = gathered(txt_own, txt_back, high)
    for copy in second[high - 1 :]:
        copy.wait_recv()
    grads_ref[0] = gathered(img_own, img_back, wide)
    each_loss(lambda copy: copy.wait_recv())
    total_ref[...] = jnp.sum(loss_buf[...], axis=0)

    for copy in first + second:
        copy.wait_send()
    each_loss(lambda copy: copy.wait_send())


def finish(pairs, grads_ref, units_ref, norms_ref, total_ref, loss_ref, gimg_ref, gtxt_ref):
    gimg_ref[...] = back_rows(units_ref[0], norms_ref[0][:, :1], grads_ref[0])
    gtxt_ref[...] = back_rows(units_ref[1], norms_ref[1][:, :1], grads_ref[1])
    loss_ref[...] = -total_ref[0, :1] / pairs


def body(images, texts, match, logit_scale, logit_bias):
    row_count = lax.axis_size("row")
    col_count = lax.axis_size("col")
    low = split_rows(row_count, col_count)
    high = row_count // low * col_count
    wide = low
    count = row_count * col_count
    shard, width = images.shape
    half = width // 2
    dma = pltpu.SemaphoreType.DMA
    vmem = pl.BlockSpec(memory_space=pltpu.VMEM)
    inputs = [pltpu.with_memory_space_constraint(images, pltpu.HBM), pltpu.with_memory_space_constraint(texts, pltpu.HBM), pltpu.with_memory_space_constraint(match, pltpu.HBM), logit_scale, logit_bias]
    sums = pl.pallas_call(
        functools.partial(exchange, low, row_count, col_count),
        out_shape=(
            jax.ShapeDtypeStruct((2, shard, width), F32),
            jax.ShapeDtypeStruct((2, shard, width), F32),
            jax.ShapeDtypeStruct((2, shard, 128), F32),
            jax.ShapeDtypeStruct((1, 128), F32),
        ),
        in_specs=[pl.BlockSpec(memory_space=pl.ANY)] * 5,
        out_specs=(vmem,) * 4,
        scratch_shapes=[
            pltpu.VMEM((shard, width), BF16),
            pltpu.VMEM((shard, width), BF16),
            pltpu.SMEM((shard,), jnp.int32),
            pltpu.SMEM((1,), F32),
            pltpu.SMEM((1,), F32),
            pltpu.VMEM((wide, 2 * shard, half + 128), BF16),
            pltpu.VMEM((high, 2 * shard, half), BF16),
            pltpu.VMEM((wide, shard, width), F32),
            pltpu.VMEM((high, shard, width), F32),
            pltpu.VMEM((wide, shard, width), F32),
            pltpu.VMEM((high, shard, width), F32),
            pltpu.VMEM((1, 128), F32),
            pltpu.VMEM((count, 1, 128), F32),
            dma((5,)),
            dma((wide,)),
            dma((wide,)),
            dma((high,)),
            dma((high,)),
            dma((wide,)),
            dma((wide,)),
            dma((high,)),
            dma((high,)),
            dma((count,)),
            dma((count,)),
        ],
        compiler_params=pltpu.CompilerParams(
            collective_id=0, has_side_effects=True, vmem_limit_bytes=32 * 1024 * 1024
        ),
    )(*inputs)
    return tuple(
        pl.pallas_call(
            functools.partial(finish, shard * count),
            out_shape=(
                jax.ShapeDtypeStruct((1,), F32),
                jax.ShapeDtypeStruct((shard, width), F32),
                jax.ShapeDtypeStruct((shard, width), F32),
            ),
            in_specs=[vmem] * 4,
            out_specs=(vmem,) * 3,
            compiler_params=pltpu.CompilerParams(vmem_limit_bytes=4 * 1024 * 1024),
        )(*sums)
    )


def solution(mesh):
    placed = (
        P(("grp", "row", "col"), None),
        P(("grp", "row", "col"), None),
        P(("grp", "row", "col")),
        P(),
        P(),
    )
    return jax.shard_map(
        body,
        mesh=mesh,
        in_specs=placed,
        out_specs=(P("grp"), P(("grp", "row", "col"), None), P(("grp", "row", "col"), None)),
        check_vma=False,
    )
```
